128 devices in a mesh: fsdp: 32 (over y_hi, z, x), tp: 4 (over y_lo, core).
Axes of the slice: x: 4, y: 4 (y_hi: 2, y_lo: 2; y = y_hi * 2 + y_lo), z: 4, core: 2. Of those that a mesh axis runs over, the one named last changes fastest.
Arguments:
- tokens: bfloat16 [16384, 1024], P(('fsdp', 'tp')), may hold values from -6 to 6
- segments: int32 [16384], P('fsdp'), may hold values from 0 to 1, as said below
- mix_gain: bfloat16 [1024], replicated, may hold values from 0.5 to 1.5
- in_weight: bfloat16 [3, 1024, 1024], P(None, 'fsdp', 'tp'), may hold values from -0.1875 to 0.1875
- conv_weight: bfloat16 [3, 1024], replicated, may hold values from -3.5 to 3.5
- out_weight: bfloat16 [1024, 1024], P('tp', 'fsdp'), may hold values from -0.1875 to 0.1875
- ffn_gain: bfloat16 [1024], replicated, may hold values from 0.5 to 1.5
- up_gate_weight: bfloat16 [2, 1024, 4608], P(None, 'fsdp', 'tp'), may hold values from -0.1875 to 0.1875
- down_weight: bfloat16 [4608, 1024], P('tp', 'fsdp'), may hold values from -0.09375 to 0.09375
- cotangent: bfloat16 [16384, 1024], P(('fsdp', 'tp')), may hold values from -24 to 24
Outputs:
- mixed: bfloat16 [16384, 1024], P(('fsdp', 'tp'))
- input_grad: float32 [16384, 1024], P(('fsdp', 'tp'))
- mix_gain_grad: float32 [1024], replicated
- in_weight_grad: float32 [3, 1024, 1024], P(None, 'fsdp', 'tp')
- conv_weight_grad: float32 [3, 1024], replicated
- out_weight_grad: float32 [1024, 1024], P('tp', 'fsdp')
- ffn_gain_grad: float32 [1024], replicated
- up_gate_grad: float32 [2, 1024, 4608], P(None, 'fsdp', 'tp')
- down_grad: float32 [4608, 1024], P('tp', 'fsdp')
The draws below stay inside these ranges and needn't reach their ends.
Inputs may be any that keep to these rules, and one draw needn't show every extreme that they name: `segments`: tokens form documents in order; each token holds its document's number modulo 2, so the value changes exactly where a document starts. Every document but the last has 200 to 2000 tokens, the last has 2 or more.
All inputs are finite; a program needn't handle non-finite values.
Results may differ from the reference program's by a relative error of at most 0.024.
Values may be sent and summed in bfloat16 or wider, within the bound.
No kernel may reach another device: no remote copies, remote signals or barrier semaphores. Data moves between devices by JAX's collectives and lax.ppermute only.
A program may use at most 128 MiB of HBM per device.

```python
from functools import partial
import jax
import jax.numpy as jnp
from jax import lax

D = 1024
FF = 4608
DOC_MIN = 200
DOC_MAX = 2000
TOKENS = 16384


def draw_segments(key, part):
    key = jax.random.fold_in(key, 11)
    count = TOKENS // DOC_MIN + 1
    doc_lengths = jax.random.randint(key, (count,), DOC_MIN, DOC_MAX + 1)
    doc_ends = jnp.cumsum(doc_lengths)
    position = jnp.arange(TOKENS, dtype=jnp.int32)
    doc_ids = jnp.searchsorted(doc_ends, position, side='right').astype(jnp.int32)
    doc_ids = jnp.minimum(doc_ids, doc_ids[TOKENS - 2])
    return (doc_ids % 2).astype(jnp.int32)


def raised(values, own_key, source, target, parts, factor):
    def block_of(dim):
        return (jnp.arange(values.shape[dim]) // (values.shape[dim] // parts)).reshape((-1,) + (1,) * (values.ndim - 1 - dim))

    first = jax.random.permutation(own_key, parts)[block_of(target)]
    second = (block_of(target) + parts // 2) % parts
    return jnp.where((block_of(source) == first) | (block_of(source) == second), factor * values, values)


def levels(rng, shape, cuts, low, top_value):
    def one(axis_at, blocks):
        steps = jax.random.uniform(jax.random.fold_in(jax.random.fold_in(rng, 6), axis_at), (blocks,), jnp.float32, low / len(cuts), top_value / len(cuts))
        return jnp.repeat(jnp.exp(steps), shape[axis_at] // blocks).reshape((-1,) + (1,) * (len(shape) - axis_at - 1))

    loudness = one(*cuts[0])
    for cut in cuts[1:]:
        loudness = loudness * one(*cut)
    return loudness


def normal_values(stream_key, dims, scale, bound, split=(), kind=jnp.bfloat16):
    entries = jax.random.normal(stream_key, dims, jnp.float32) * scale
    if len(split) > 0:
        entries = levels(stream_key, dims, split, -0.22, 0.18) * entries
    return jnp.clip(entries, min=-bound, max=bound).astype(kind)


def heavy_noise(rng, shape, spread, reach, shards, heavy, held_as=jnp.bfloat16):
    entries = spread * jax.random.normal(rng, shape, jnp.float32)
    if shards:
        entries = entries * levels(rng, shape, shards, -0.22, 0.18)
    return jnp.clip(raised(entries, jax.random.fold_in(rng, 3), *heavy), -reach, reach).astype(held_as)


def setup_inputs(seed: int = 0) -> dict:
    arg_keys = jax.random.split(jax.random.key(seed), 11)
    return {
        "tokens": normal_values(arg_keys[0], (TOKENS, D), 1.0, 6.0, ((0, 128),)),
        "segments": draw_segments(jax.random.fold_in(arg_keys[10], 71), 0),
        "mix_gain": jnp.clip(1.0 + 0.1 * jax.random.normal(arg_keys[2], (D,), jnp.float32), 0.5, 1.5).astype(jnp.bfloat16),
        "in_weight": normal_values(arg_keys[3], (3, D, D), D ** -0.5, 0.1875, ((1, 32), (2, 4))),
        "conv_weight": normal_values(arg_keys[4], (3, D), 3 ** -0.5, 3.5),
        "out_weight": normal_values(arg_keys[5], (D, D), D ** -0.5, 0.1875, ((0, 4), (1, 32))),
        "ffn_gain": jnp.clip(1.0 + 0.1 * jax.random.normal(arg_keys[6], (D,), jnp.float32), 0.5, 1.5).astype(jnp.bfloat16),
        "up_gate_weight": normal_values(arg_keys[7], (2, D, FF), D ** -0.5, 0.1875, ((1, 32), (2, 4))),
        "down_weight": normal_values(arg_keys[8], (FF, D), FF ** -0.5, 0.09375, ((0, 4), (1, 32))),
        "cotangent": heavy_noise(arg_keys[9], (TOKENS, D), 1.0, 24.0, ((0, 128),), (0, 1, 128, 5.5)),
    }


@jax.custom_vjp
def low(v):
    return lax.optimization_barrier(v.astype(jnp.bfloat16)).astype(jnp.float32)

@jax.custom_vjp
def low_back(v):
    return v

def low_keep(v):
    return (low(v), None)

def low_pass(kept, grad):
    return (grad,)

def back_keep(v):
    return (v, None)

def back_low(kept, grad):
    return (low(grad),)
low.defvjp(low_keep, low_pass)
low_back.defvjp(back_keep, back_low)
EPSILON = 1e-05

def matmul(left, right):
    return jnp.dot(left, right, precision=lax.Precision.HIGHEST)

def rms_norm(values, weight):
    return values * lax.rsqrt(lax.optimization_barrier(jnp.mean(values * values, axis=-1, keepdims=True)) + EPSILON) * weight

def feed_block(rows_in, ffn_gain, up_gate, down_weight):
    normed = low(rms_norm(rows_in, ffn_gain))
    gate_pre = low_back(matmul(normed, up_gate[0]))
    up_pre = low_back(matmul(normed, up_gate[1]))
    hidden = low(jax.nn.silu(gate_pre) * up_pre)
    return low_back(matmul(hidden, down_weight))

def forward(segments, tok_in, mix_gain, in_weight, conv_weight, out_weight, ffn_gain, up_gate, down_weight):
    normed = low(rms_norm(tok_in, mix_gain))
    proj_b = low_back(low(matmul(normed, in_weight[0])))
    proj_c = low_back(low(matmul(normed, in_weight[1])))
    proj_x = low_back(low(matmul(normed, in_weight[2])))
    product = proj_b * proj_x
    padded = jnp.concatenate([jnp.zeros((2, D), jnp.float32), product], axis=0)
    seg_pad = jnp.concatenate([jnp.full((2,), -1, jnp.int32), segments.astype(jnp.int32)])
    conv_out = jnp.zeros_like(product)
    for offset in range(3):
        same_doc = (seg_pad[2 - offset:2 - offset + TOKENS] == segments).astype(jnp.float32)
        conv_out = conv_out + conv_weight[2 - offset] * same_doc[:, None] * padded[2 - offset:2 - offset + TOKENS]
    mixer_in = low(proj_c * conv_out)
    middle = tok_in + low_back(matmul(mixer_in, out_weight))
    blocks_n = max(TOKENS // 4096, 1)
    blocks = middle.reshape(blocks_n, TOKENS // blocks_n, D)
    step_fn = jax.checkpoint(lambda rows_in: feed_block(rows_in, ffn_gain, up_gate, down_weight))
    ffn_out = lax.map(step_fn, blocks).reshape(TOKENS, D)
    return middle + ffn_out

def reference(tokens, segments, mix_gain, in_weight, conv_weight, out_weight, ffn_gain, up_gate_weight, down_weight, cotangent):
    params = [tokens.astype(jnp.float32), mix_gain.astype(jnp.float32), in_weight.astype(jnp.float32), conv_weight.astype(jnp.float32), out_weight.astype(jnp.float32), ffn_gain.astype(jnp.float32), up_gate_weight.astype(jnp.float32), down_weight.astype(jnp.float32)]
    result, pullback = jax.vjp(partial(forward, segments), *params)
    grads = pullback(cotangent.astype(jnp.float32))
    return (result.astype(jnp.bfloat16), grads[0], grads[1], grads[2], grads[3], grads[4], grads[5], grads[6], grads[7])
```

```python
import jax
import jax.numpy as jnp
from jax import lax
from jax.sharding import Mesh, PartitionSpec as P

EPSILON = 1e-05
F32 = jnp.float32
BF16 = jnp.bfloat16
FSDP = ("yh", "z", "x")
TP = ("yl", "core")
ALL = FSDP + TP


def dot(lhs, rhs, lhs_dim, rhs_dim):
    return lax.dot_general(
        lhs, rhs, (((lhs_dim,), (rhs_dim,)), ((), ())), preferred_element_type=F32
    )


def shifted(value, axis, by):
    size = lax.axis_size(axis)
    return lax.ppermute(value, axis, [(i, (i + by) % size) for i in range(size)])


def swapped(value, axis):
    return lax.ppermute(value, axis, [(0, 1), (1, 0)])


def norm_parts(values):
    scale = lax.rsqrt(jnp.mean(values * values, axis=-1, keepdims=True) + EPSILON)
    return (scale, values * scale)


def norm_back(grad_out, gain, scale, normed):
    grad_norm = grad_out * gain
    return scale * (grad_norm - normed * jnp.mean(grad_norm * normed, axis=-1, keepdims=True))


def put(block, whole, dim, index):
    return lax.dynamic_update_slice_in_dim(whole, jnp.expand_dims(block, dim), index, dim)


def take(whole, dim, index):
    return lax.dynamic_index_in_dim(whole, index, dim, keepdims=False)


def ring_gather(block, axis, dim):
    me = lax.axis_index(axis)
    shape = block.shape[:dim] + (4,) + block.shape[dim:]
    whole = jnp.zeros(shape, block.dtype)
    whole = put(block, whole, dim, me)
    for by in (1, 3, 2):
        whole = put(shifted(block, axis, by), whole, dim, (me - by) % 4)
    return whole


def ring_scatter(whole, axis, dim):
    me = lax.axis_index(axis)
    total = take(whole, dim, me).astype(F32)
    for by in (1, 3, 2):
        total = total + shifted(take(whole, dim, (me + by) % 4), axis, by).astype(F32)
    return total


def gather_rows(shard):
    rows, columns = shard.shape
    other = swapped(shard, "yh")
    first = lax.axis_index("yh") == 0
    pair = jnp.stack([jnp.where(first, shard, other), jnp.where(first, other, shard)])
    half = rows // 2
    upper, lower = pair[:, :half], pair[:, half:]
    upper = ring_gather(upper, "z", 1)
    lower = ring_gather(lower, "x", 1)
    upper = ring_gather(upper, "x", 2)
    lower = ring_gather(lower, "z", 1)
    return jnp.stack([upper, lower], axis=3).reshape(32 * rows, columns)


def scatter_rows(whole):
    columns = whole.shape[1]
    parts = whole.reshape(2, 4, 4, 2, -1, columns)
    upper, lower = parts[:, :, :, 0], parts[:, :, :, 1]
    upper = ring_scatter(upper, "x", 2).astype(BF16)
    lower = ring_scatter(lower, "z", 1).astype(BF16)
    upper = ring_scatter(upper, "z", 1)
    lower = ring_scatter(lower, "x", 1)
    pair = jnp.concatenate([upper, lower], axis=1)
    me = lax.axis_index("yh")
    return take(pair, 0, me) + swapped(take(pair, 0, 1 - me).astype(BF16), "yh").astype(F32)


def gather_tokens(block):
    core = lax.axis_index("core") == 0
    lane = lax.axis_index("yl") == 0

    def ordered(first, mine, other):
        return [jnp.where(first, mine, other), jnp.where(first, other, mine)]

    far = swapped(block, "yl")
    near = jnp.concatenate(ordered(core, block, swapped(block, "core")))
    beyond = jnp.concatenate(ordered(core, far, swapped(far, "core")))
    return jnp.concatenate(ordered(lane, near, beyond))


def scatter_tokens(terms):
    core = lax.axis_index("core")
    lane = lax.axis_index("yl")
    blocks = terms.reshape(2, 2, -1, terms.shape[1])
    sent = take(blocks, 1, 1 - core).astype(BF16)
    pair = take(blocks, 1, core).astype(F32) + swapped(sent, "core").astype(F32)
    sent = take(pair, 0, 1 - lane).astype(BF16)
    return take(pair, 0, lane) + swapped(sent, "yl").astype(F32)


def sum_everywhere(value):
    value = value + swapped(value, "core")
    value = value + swapped(value, "yl")
    value = value + swapped(value, "yh")
    for axis in ("x", "z"):
        value = (value + shifted(value, axis, 2)) + (
            shifted(value, axis, 1) + shifted(value, axis, 3)
        )
    return value


def along_tokens(value, by):
    pairs = [(i, i + by) for i in range(32) if 0 <= i + by < 32]
    return lax.ppermute(value, FSDP, pairs)


def local(
    tokens,
    segments,
    mix_gain,
    in_weight,
    conv_weight,
    out_weight,
    ffn_gain,
    up_gate_weight,
    down_weight,
    cotangent,
):
    width = tokens.shape[1]
    chan_dev = in_weight.shape[2]
    hidden_dev = up_gate_weight.shape[2]
    shard_rows = in_weight.shape[1]
    tp_index = lax.axis_index("yl") * 2 + lax.axis_index("core")

    in_rows = jnp.concatenate([in_weight[0], in_weight[1], in_weight[2]], axis=1)
    in_full = gather_rows(in_rows)
    mid_rows = jnp.concatenate([out_weight.T, up_gate_weight[0], up_gate_weight[1]], axis=1)
    mid_full = gather_rows(mid_rows)
    out_full = mid_full[:, :chan_dev]
    gate_full = mid_full[:, chan_dev:]
    down_full = gather_rows(down_weight.T)

    conv_local = lax.dynamic_slice_in_dim(conv_weight, tp_index * chan_dev, chan_dev, 1).astype(F32)
    tok_f32 = tokens.astype(F32)
    scale_one, normed_one = norm_parts(tok_f32)
    gain_one = mix_gain.astype(F32)
    mix_rows = gather_tokens((normed_one * gain_one).astype(BF16))
    group_rows = mix_rows.shape[0]
    projected = dot(mix_rows, in_full, 1, 0).astype(BF16)
    proj_b = projected[:, :chan_dev].astype(F32)
    proj_c = projected[:, chan_dev : 2 * chan_dev].astype(F32)
    proj_x = projected[:, 2 * chan_dev :].astype(F32)
    product = proj_b * proj_x
    parity = (segments % 2).astype(F32)
    parity_row = jnp.zeros((1, chan_dev), F32).at[0, :2].set(parity[-2:])
    rim_send = jnp.concatenate([product[-2:], parity_row], axis=0)
    rim_recv = along_tokens(rim_send, 1)
    padded = jnp.concatenate([rim_recv[:2], product], axis=0)
    parity_pad = jnp.concatenate([rim_recv[2, :2], parity])
    masks = [
        (parity_pad[2 - offset : 2 - offset + group_rows] == parity).astype(F32)[:, None]
        for offset in range(3)
    ]
    conv_out = jnp.zeros_like(product)
    for offset in range(3):
        conv_out = (
            conv_out
            + conv_local[2 - offset] * masks[offset] * padded[2 - offset : 2 - offset + group_rows]
        )
    mixer_in = (proj_c * conv_out).astype(BF16)
    middle = tok_f32 + scatter_tokens(dot(mixer_in, out_full, 1, 1))
    scale_two, normed_two = norm_parts(middle)
    gain_two = ffn_gain.astype(F32)
    ffn_rows = gather_tokens((normed_two * gain_two).astype(BF16))
    cot_rows = gather_tokens(cotangent)
    grad_hidden = dot(cot_rows, down_full, 1, 0)
    gate_up = dot(ffn_rows, gate_full, 1, 0)
    gate_val = gate_up[:, :hidden_dev]
    up_val = gate_up[:, hidden_dev:]
    sigma = jax.nn.sigmoid(gate_val)
    hidden = (gate_val * sigma * up_val).astype(BF16)
    grad_up = grad_hidden * gate_val * sigma
    grad_gate = grad_hidden * up_val * sigma * (1.0 + gate_val * (1.0 - sigma))
    grad_pair = jnp.concatenate([grad_gate.astype(BF16), grad_up.astype(BF16)], axis=1)
    grad_normed_two = scatter_tokens(dot(grad_pair, gate_full, 1, 1))
    grad_down = dot(cot_rows, hidden, 0, 0).astype(BF16)
    grad_gate_w = dot(ffn_rows, grad_pair, 0, 0).astype(BF16)
    mixed = (middle + scatter_tokens(dot(hidden, down_full, 1, 1))).astype(BF16)

    gain_two_grad = jnp.sum(grad_normed_two * normed_two, axis=0)
    grad_middle = cotangent.astype(F32) + norm_back(grad_normed_two, gain_two, scale_two, normed_two)
    grad_mix_rows = gather_tokens(grad_middle.astype(BF16))
    grad_mixer_in = dot(grad_mix_rows, out_full, 1, 0)
    grad_out_w = dot(grad_mix_rows, mixer_in, 0, 0).astype(BF16)
    grad_c = grad_mixer_in * conv_out
    grad_conv = grad_mixer_in * proj_c
    grad_padded = jnp.zeros((group_rows + 2, chan_dev), F32)
    conv_grads = []
    for offset in range(3):
        masked = masks[offset] * grad_conv
        grad_padded = grad_padded + jnp.pad(
            conv_local[2 - offset] * masked, ((2 - offset, offset), (0, 0))
        )
        conv_grads.append(jnp.sum(masked * padded[2 - offset : 2 - offset + group_rows], axis=0))
    conv_grad_local = jnp.stack([conv_grads[2], conv_grads[1], conv_grads[0]])
    rim_back = along_tokens(grad_padded[:2], -1)
    grad_product = grad_padded[2:] + jnp.pad(rim_back, ((group_rows - 2, 0), (0, 0)))
    grad_proj = jnp.concatenate(
        [
            (grad_product * proj_x).astype(BF16),
            grad_c.astype(BF16),
            (grad_product * proj_b).astype(BF16),
        ],
        axis=1,
    )
    grad_in_w = dot(mix_rows, grad_proj, 0, 0).astype(BF16)
    grad_normed_one = scatter_tokens(dot(grad_proj, in_full, 1, 1))
    gain_one_grad = jnp.sum(grad_normed_one * normed_one, axis=0)
    input_grad = grad_middle + norm_back(grad_normed_one, gain_one, scale_one, normed_one)

    down_shard = scatter_rows(grad_down)
    gate_shard = scatter_rows(grad_gate_w)
    last_shard = scatter_rows(jnp.concatenate([grad_out_w, grad_in_w], axis=1))
    out_shard = last_shard[:, :chan_dev]
    in_shard = last_shard[:, chan_dev:]

    conv_full = lax.dynamic_update_slice_in_dim(
        jnp.zeros((3, width), F32), conv_grad_local, tp_index * chan_dev, 1
    )
    sums = sum_everywhere(
        jnp.concatenate([gain_one_grad[None], gain_two_grad[None], conv_full], axis=0)
    )
    return (
        mixed,
        input_grad,
        sums[0],
        jnp.stack([in_shard[:, i * chan_dev : (i + 1) * chan_dev] for i in range(3)]),
        sums[2:],
        out_shard.T,
        sums[1],
        jnp.stack([gate_shard[:, :hidden_dev], gate_shard[:, hidden_dev:]]),
        down_shard.T,
    )


def solution(mesh):
    fine = Mesh(mesh.devices.reshape(2, 4, 4, 2, 2), ALL)
    placed = (
        P(ALL, None),
        P(FSDP),
        P(),
        P(None, FSDP, TP),
        P(),
        P(TP, FSDP),
        P(),
        P(None, FSDP, TP),
        P(TP, FSDP),
        P(ALL, None),
    )
    return jax.shard_map(
        local,
        mesh=fine,
        in_specs=placed,
        out_specs=(
            P(ALL, None),
            P(ALL, None),
            P(),
            P(None, FSDP, TP),
            P(),
            P(TP, FSDP),
            P(),
            P(None, FSDP, TP),
            P(TP, FSDP),
        ),
        check_vma=False,
    )
```

```python
import jax
import jax.numpy as jnp
from jax import lax
from jax.sharding import Mesh, PartitionSpec as P

EPSILON = 1e-05
F32 = jnp.float32
BF16 = jnp.bfloat16
FSDP = ("yh", "z", "x")
TP = ("yl", "core")
ALL = FSDP + TP


def dot(lhs, rhs, lhs_dim, rhs_dim):
    return lax.dot_general(
        lhs, rhs, (((lhs_dim,), (rhs_dim,)), ((), ())), preferred_element_type=F32
    )


def shifted(value, axis, by):
    size = lax.axis_size(axis)
    return lax.ppermute(value, axis, [(i, (i + by) % size) for i in range(size)])


def swapped(value, axis):
    return lax.ppermute(value, axis, [(0, 1), (1, 0)])


def norm_parts(values):
    scale = lax.rsqrt(jnp.mean(values * values, axis=-1, keepdims=True) + EPSILON)
    return (scale, values * scale)


def norm_back(grad_out, gain, scale, normed):
    grad_norm = grad_out * gain
    return scale * (grad_norm - normed * jnp.mean(grad_norm * normed, axis=-1, keepdims=True))


def after(value, *earlier):
    return lax.optimization_barrier((value,) + earlier)[0]


def no_sooner(value, earlier):
    corner = lax.slice(earlier, (0,) * earlier.ndim, (1,) * earlier.ndim).reshape(())
    return value + jnp.minimum(jnp.abs(corner), 0).astype(value.dtype)


def put(block, whole, dim, index):
    return lax.dynamic_update_slice_in_dim(whole, jnp.expand_dims(block, dim), index, dim)


def take(whole, dim, index):
    return lax.dynamic_index_in_dim(whole, index, dim, keepdims=False)


def ring_gather(block, axis, dim):
    me = lax.axis_index(axis)
    whole = jnp.zeros(block.shape[:dim] + (4,) + block.shape[dim:], block.dtype)
    whole = put(block, whole, dim, me)
    for by in (1, 3, 2):
        whole = put(shifted(block, axis, by), whole, dim, (me - by) % 4)
    return whole


def ring_gather_passing(block, axis, dim):
    me = lax.axis_index(axis)
    before = shifted(block, axis, 1)
    behind = shifted(block, axis, -1)
    far = jnp.concatenate([shifted(before[:1], axis, 1), shifted(behind[1:], axis, -1)])
    whole = jnp.zeros(block.shape[:dim] + (4,) + block.shape[dim:], block.dtype)
    for value, by in ((block, 0), (before, 3), (behind, 1), (far, 2)):
        whole = put(value, whole, dim, (me + by) % 4)
    return whole


def pair_rows(shard):
    other = swapped(shard, "yh")
    first = lax.axis_index("yh") == 0
    return jnp.stack([jnp.where(first, shard, other), jnp.where(first, other, shard)])


def gather_rows(first, second):
    pair = pair_rows(jnp.concatenate([first, second], axis=1))
    columns = first.shape[1]
    one = ring_gather(ring_gather(pair[:, :, :columns], "z", 1), "x", 2)
    two = ring_gather_passing(ring_gather(pair[:, :, columns:], "x", 1), "z", 1)
    return one.reshape(-1, columns), two.reshape(-1, second.shape[1])


def ring_scatter_passing(whole, axis, dim, *earlier):
    me = lax.axis_index(axis)
    far = take(whole, dim, (me + 2) % 4)
    up, down = shifted(far[:1], axis, 1), shifted(far[1:], axis, -1)
    if earlier:
        up, down = after(up, *earlier), after(down, *earlier)
    rest = [(0, 0)] * (far.ndim - 1)
    ahead = take(whole, dim, (me + 1) % 4).astype(F32) + jnp.pad(up.astype(F32), [(0, 1)] + rest)
    back = take(whole, dim, (me + 3) % 4).astype(F32) + jnp.pad(down.astype(F32), [(1, 0)] + rest)
    ahead, back = shifted(ahead.astype(BF16), axis, 1), shifted(back.astype(BF16), axis, -1)

    def finish(earlier):
        total = no_sooner(take(whole, dim, me).astype(F32), earlier)
        return total + ahead.astype(F32) + back.astype(F32)

    return finish


def ring_scatter(whole, axis, dim):
    me = lax.axis_index(axis)
    total = take(whole, dim, me).astype(F32)
    for by in (1, 3, 2):
        total = total + shifted(take(whole, dim, (me + by) % 4), axis, by).astype(F32)
    return total


def pair_scatter(whole):
    me = lax.axis_index("yh")
    return take(whole, 0, me) + swapped(take(whole, 0, 1 - me).astype(BF16), "yh").astype(F32)


def exchange_sum(whole, axes):
    count = 1
    for axis in axes:
        count *= lax.axis_size(axis)
    parts = lax.all_to_all(whole.reshape(count, -1, whole.shape[1]), axes, 0, 0)
    return jnp.sum(parts.astype(F32), axis=0)


def yh_innermost(rows):
    parts = rows.reshape(rows.shape[0], 2, 16, -1).swapaxes(1, 2)
    return parts.reshape(rows.shape)


def gather_tokens(block):
    pair = jnp.concatenate([block, swapped(block, "yl")])
    return jnp.concatenate([pair, swapped(pair, "core")])


def scatter_tokens(terms):
    half = terms.shape[0] // 2
    pair = terms[:half].astype(F32) + swapped(terms[half:].astype(BF16), "core").astype(F32)
    rows = half // 2
    return pair[:rows] + swapped(pair[rows:].astype(BF16), "yl").astype(F32)


def reordered(rows):
    blocks = rows.reshape(4, -1, rows.shape[1])
    me = lax.axis_index("core") * 2 + lax.axis_index("yl")
    return jnp.concatenate([take(blocks, 0, me ^ other) for other in (0, 2, 1, 3)])


def restored(rows):
    blocks = rows.reshape(4, -1, rows.shape[1])
    me = lax.axis_index("yl") * 2 + lax.axis_index("core")
    return jnp.concatenate([take(blocks, 0, me ^ other) for other in (0, 2, 1, 3)])


def along_tokens(value, by):
    pairs = [(i, i + by) for i in range(32) if 0 <= i + by < 32]
    return lax.ppermute(value, FSDP, pairs)


def local(
    tokens,
    segments,
    mix_gain,
    in_weight,
    conv_weight,
    out_weight,
    ffn_gain,
    up_gate_weight,
    down_weight,
    cotangent,
):
    width = tokens.shape[1]
    chan_dev = in_weight.shape[2]
    hidden_dev = up_gate_weight.shape[2]
    shard_rows = in_weight.shape[1]
    tp_index = lax.axis_index("yl") * 2 + lax.axis_index("core")

    in_shard = jnp.concatenate([in_weight[0], in_weight[1], in_weight[2]], axis=1)
    in_full, second_full = gather_rows(
        in_shard, jnp.concatenate([out_weight.T, down_weight.T], axis=1)
    )
    out_full = second_full[:, :chan_dev]
    down_full = second_full[:, chan_dev:]
    up_gate_full = lax.all_gather(up_gate_weight, FSDP, axis=1, tiled=True)

    conv_local = lax.dynamic_slice_in_dim(conv_weight, tp_index * chan_dev, chan_dev, 1).astype(F32)
    tok_f32 = tokens.astype(F32)
    scale_one, normed_one = norm_parts(tok_f32)
    gain_one = mix_gain.astype(F32)
    mix_rows = reordered(gather_tokens((normed_one * gain_one).astype(BF16)))
    group_rows = mix_rows.shape[0]
    projected = dot(mix_rows, in_full, 1, 0).astype(BF16)
    proj_b = projected[:, :chan_dev].astype(F32)
    proj_c = projected[:, chan_dev : 2 * chan_dev].astype(F32)
    proj_x = projected[:, 2 * chan_dev :].astype(F32)
    product = proj_b * proj_x
    parity = (segments % 2).astype(F32)
    parity_row = jnp.zeros((1, chan_dev), F32).at[0, :2].set(parity[-2:])
    rim_send = jnp.concatenate([product[-2:], parity_row], axis=0)
    rim_recv = along_tokens(rim_send, 1)
    padded = jnp.concatenate([rim_recv[:2], product], axis=0)
    parity_pad = jnp.concatenate([rim_recv[2, :2], parity])
    masks = [
        (parity_pad[2 - offset : 2 - offset + group_rows] == parity).astype(F32)[:, None]
        for offset in range(3)
    ]
    conv_out = jnp.zeros_like(product)
    for offset in range(3):
        conv_out = (
            conv_out
            + conv_local[2 - offset] * masks[offset] * padded[2 - offset : 2 - offset + group_rows]
        )
    mixer_in = (proj_c * conv_out).astype(BF16)
    mixer_out = scatter_tokens(dot(restored(mixer_in), out_full, 1, 1))
    middle = tok_f32 + after(mixer_out, up_gate_full)
    scale_two, normed_two = norm_parts(middle)
    gain_two = ffn_gain.astype(F32)
    cot_rows = gather_tokens(after(cotangent, mix_rows))
    ffn_rows = gather_tokens((normed_two * gain_two).astype(BF16))
    grad_hidden = dot(cot_rows, down_full, 1, 0)
    gate_val = dot(ffn_rows, up_gate_full[0], 1, 0)
    up_val = dot(ffn_rows, up_gate_full[1], 1, 0)
    sigma = jax.nn.sigmoid(gate_val)
    hidden = (gate_val * sigma * up_val).astype(BF16)
    grad_up = grad_hidden * gate_val * sigma
    grad_gate = grad_hidden * up_val * sigma * (1.0 + gate_val * (1.0 - sigma))
    grad_gate = grad_gate.astype(BF16)
    grad_up = grad_up.astype(BF16)
    grad_down = dot(yh_innermost(cot_rows), hidden, 0, 0).astype(BF16)
    down_pair = lax.psum_scatter(grad_down, ("z", "x"), scatter_dimension=0, tiled=True)
    grad_gate = after(grad_gate, grad_down)
    grad_rows_two = dot(grad_gate, up_gate_full[0], 1, 1) + dot(grad_up, up_gate_full[1], 1, 1)
    grad_gate_w = dot(
        after(ffn_rows, grad_rows_two), jnp.concatenate([grad_gate, grad_up], axis=1), 0, 0
    ).astype(BF16)
    grad_normed_two = scatter_tokens(grad_rows_two)
    gain_two_grad = jnp.sum(grad_normed_two * normed_two, axis=0)
    grad_middle = cotangent.astype(F32) + norm_back(grad_normed_two, gain_two, scale_two, normed_two)
    grad_mid_low = grad_middle.astype(BF16)
    grad_mix_rows = reordered(gather_tokens(grad_mid_low))
    by_z = ring_scatter_passing(
        grad_gate_w.reshape(2, 4, 4, shard_rows, -1), "z", 1, grad_mid_low
    )
    ffn_terms = dot(after(hidden, grad_mid_low), down_full, 1, 1)
    mixed = (middle + scatter_tokens(after(ffn_terms, grad_mix_rows))).astype(BF16)
    grad_mixer_in = dot(grad_mix_rows, out_full, 1, 0)
    grad_out_w = dot(grad_mix_rows, mixer_in, 0, 0).astype(BF16)
    grad_c = grad_mixer_in * conv_out
    grad_conv = grad_mixer_in * proj_c
    grad_padded = jnp.zeros((group_rows + 2, chan_dev), F32)
    conv_grads = []
    for offset in range(3):
        masked = masks[offset] * grad_conv
        grad_padded = grad_padded + jnp.pad(
            conv_local[2 - offset] * masked, ((2 - offset, offset), (0, 0))
        )
        conv_grads.append(jnp.sum(masked * padded[2 - offset : 2 - offset + group_rows], axis=0))
    conv_grad_local = jnp.stack([conv_grads[2], conv_grads[1], conv_grads[0]])
    rim_back = along_tokens(grad_padded[:2], -1)
    grad_product = grad_padded[2:] + jnp.pad(rim_back, ((group_rows - 2, 0), (0, 0)))
    grad_proj = jnp.concatenate(
        [
            (grad_product * proj_x).astype(BF16),
            grad_c.astype(BF16),
            (grad_product * proj_b).astype(BF16),
        ],
        axis=1,
    )
    grad_in_w = dot(mix_rows, grad_proj, 0, 0).astype(BF16)
    grad_rows_one = dot(grad_proj, in_full, 1, 1)
    gain_one_grad = jnp.sum(grad_rows_one * mix_rows.astype(F32), axis=0) / gain_one
    grad_normed_one = scatter_tokens(restored(grad_rows_one))
    input_grad = grad_middle + norm_back(grad_normed_one, gain_one, scale_one, normed_one)

    small = jnp.concatenate(
        [
            gain_one_grad.reshape(shard_rows, -1),
            gain_two_grad.reshape(shard_rows, -1),
            conv_grad_local.reshape(shard_rows, -1),
        ],
        axis=1,
    )
    small = jnp.pad(small, ((0, 0), (0, 128 - small.shape[1]))).astype(BF16)
    small = jnp.broadcast_to(small, (32,) + small.shape).reshape(width, 128)
    last_grad = jnp.concatenate([grad_out_w, grad_in_w, small], axis=1)
    last_shard = exchange_sum(last_grad, FSDP)
    by_z = by_z(grad_in_w).astype(BF16)
    ffn_grad_shard = pair_scatter(
        jnp.concatenate(
            [
                ring_scatter(by_z, "x", 1),
                down_pair.reshape(2, shard_rows, hidden_dev).astype(F32),
            ],
            axis=2,
        )
    )
    down_shard = ffn_grad_shard[:, 2 * hidden_dev :]
    gate_shard = ffn_grad_shard[:, :hidden_dev]
    up_shard = ffn_grad_shard[:, hidden_dev : 2 * hidden_dev]
    out_shard = last_shard[:, :chan_dev]
    in_shard = last_shard[:, chan_dev : 4 * chan_dev]
    sums = last_shard[:, 4 * chan_dev :]
    per = width // shard_rows
    conv_sum = sums[:, 2 * per : 2 * per + 3 * chan_dev // shard_rows].reshape(3, chan_dev)
    conv_sum = lax.dynamic_update_slice_in_dim(
        jnp.zeros((3, width), F32), conv_sum, tp_index * chan_dev, 1
    )
    sums = jnp.concatenate(
        [sums[:, :per].reshape(1, width), sums[:, per : 2 * per].reshape(1, width), conv_sum]
    )
    sums = sums + swapped(sums, "core")
    sums = sums + swapped(sums, "yl")
    return (
        mixed,
        input_grad,
        sums[0],
        jnp.stack([in_shard[:, i * chan_dev : (i + 1) * chan_dev] for i in range(3)]),
        sums[2:],
        out_shard.T,
        sums[1],
        jnp.stack([gate_shard, up_shard]),
        down_shard.T,
    )


def solution(mesh):
    fine = Mesh(mesh.devices.reshape(2, 4, 4, 2, 2), ALL)
    placed = (
        P(ALL, None),
        P(FSDP),
        P(),
        P(None, FSDP, TP),
        P(),
        P(TP, FSDP),
        P(),
        P(None, FSDP, TP),
        P(TP, FSDP),
        P(ALL, None),
    )
    return jax.shard_map(
        local,
        mesh=fine,
        in_specs=placed,
        out_specs=(
            P(ALL, None),
            P(ALL, None),
            P(),
            P(None, FSDP, TP),
            P(),
            P(TP, FSDP),
            P(),
            P(None, FSDP, TP),
            P(TP, FSDP),
        ),
        check_vma=False,
    )
```

```python
import jax
import jax.numpy as jnp
from jax import lax
from jax.sharding import Mesh, PartitionSpec as P

EPSILON = 1e-05
F32 = jnp.float32
BF16 = jnp.bfloat16
FSDP = ("yh", "z", "x")
TP = ("yl", "core")
ALL = FSDP + TP


def dot(lhs, rhs, lhs_dim, rhs_dim):
    return lax.dot_general(
        lhs, rhs, (((lhs_dim,), (rhs_dim,)), ((), ())), preferred_element_type=F32
    )


def shifted(value, axis, by):
    size = lax.axis_size(axis)
    return lax.ppermute(value, axis, [(i, (i + by) % size) for i in range(size)])


def swapped(value, axis):
    return lax.ppermute(value, axis, [(0, 1), (1, 0)])


def norm_parts(values):
    scale = lax.rsqrt(jnp.mean(values * values, axis=-1, keepdims=True) + EPSILON)
    return (scale, values * scale)


def norm_back(grad_out, gain, scale, normed):
    grad_norm = grad_out * gain
    return scale * (grad_norm - normed * jnp.mean(grad_norm * normed, axis=-1, keepdims=True))


def after(value, *earlier):
    return lax.optimization_barrier((value,) + earlier)[0]


def no_sooner(value, earlier):
    corner = lax.slice(earlier, (0,) * earlier.ndim, (1,) * earlier.ndim).reshape(())
    return value + jnp.minimum(jnp.abs(corner), 0).astype(value.dtype)


def put(block, whole, dim, index):
    return lax.dynamic_update_slice_in_dim(whole, jnp.expand_dims(block, dim), index, dim)


def take(whole, dim, index):
    return lax.dynamic_index_in_dim(whole, index, dim, keepdims=False)


def ring_gather(block, axis, dim):
    me = lax.axis_index(axis)
    whole = jnp.zeros(block.shape[:dim] + (4,) + block.shape[dim:], block.dtype)
    whole = put(block, whole, dim, me)
    for by in (1, 3, 2):
        whole = put(shifted(block, axis, by), whole, dim, (me - by) % 4)
    return whole


def ring_gather_passing(block, axis, dim):
    me = lax.axis_index(axis)
    before = shifted(block, axis, 1)
    behind = shifted(block, axis, -1)
    far = jnp.concatenate([shifted(before[:1], axis, 1), shifted(behind[1:], axis, -1)])
    whole = jnp.zeros(block.shape[:dim] + (4,) + block.shape[dim:], block.dtype)
    for value, by in ((block, 0), (before, 3), (behind, 1), (far, 2)):
        whole = put(value, whole, dim, (me + by) % 4)
    return whole


def pair_rows(shard):
    other = swapped(shard, "yh")
    first = lax.axis_index("yh") == 0
    return jnp.stack([jnp.where(first, shard, other), jnp.where(first, other, shard)])


def gather_rows(first, second):
    pair = pair_rows(jnp.concatenate([first, second], axis=1))
    columns = first.shape[1]
    one = ring_gather(ring_gather(pair[:, :, :columns], "z", 1), "x", 2)
    two = ring_gather_passing(ring_gather(pair[:, :, columns:], "x", 1), "z", 1)
    return one.reshape(-1, columns), two.reshape(-1, second.shape[1])


def ring_scatter(whole, axis, dim, earlier):
    me = lax.axis_index(axis)
    total = take(whole, dim, me).astype(F32)
    for by in (1, 3, 2):
        part = no_sooner(take(whole, dim, (me + by) % 4), earlier)
        total = total + shifted(part, axis, by).astype(F32)
    return total


def exchange_sum(whole, axes):
    count = 1
    for axis in axes:
        count *= lax.axis_size(axis)
    parts = lax.all_to_all(whole.reshape(count, -1, whole.shape[1]), axes, 0, 0)
    return jnp.sum(parts.astype(F32), axis=0)


def x_outermost(rows):
    parts = rows.reshape(rows.shape[0], 2, 4, 4, -1).transpose(0, 3, 2, 1, 4)
    return parts.reshape(rows.shape)


def z_outermost(rows):
    parts = rows.reshape(rows.shape[0], 2, 4, 4, -1).swapaxes(1, 2)
    return parts.reshape(rows.shape)


def gather_tokens(block):
    return gather_core(block, swapped(block, "yl"))


def gather_core(block, far):
    pair = jnp.concatenate([block, far])
    return jnp.concatenate([pair, swapped(pair, "core")])


def scatter_tokens(terms, earlier=None):
    half = terms.shape[0] // 2
    pair = terms[:half].astype(F32) + swapped(terms[half:].astype(BF16), "core").astype(F32)
    rows = half // 2
    far = swapped(pair[rows:].astype(BF16), "yl")
    if earlier is not None:
        far = no_sooner(far, earlier)
    return pair[:rows] + far.astype(F32)


def reordered(rows):
    blocks = rows.reshape(4, -1, rows.shape[1])
    me = lax.axis_index("core") * 2 + lax.axis_index("yl")
    return jnp.concatenate([take(blocks, 0, me ^ other) for other in (0, 2, 1, 3)])


def restored(rows):
    blocks = rows.reshape(4, -1, rows.shape[1])
    me = lax.axis_index("yl") * 2 + lax.axis_index("core")
    return jnp.concatenate([take(blocks, 0, me ^ other) for other in (0, 2, 1, 3)])


def along_tokens(value, by):
    pairs = [(i, i + by) for i in range(32) if 0 <= i + by < 32]
    return lax.ppermute(value, FSDP, pairs)


def local(
    tokens,
    segments,
    mix_gain,
    in_weight,
    conv_weight,
    out_weight,
    ffn_gain,
    up_gate_weight,
    down_weight,
    cotangent,
):
    width = tokens.shape[1]
    chan_dev = in_weight.shape[2]
    hidden_dev = up_gate_weight.shape[2]
    shard_rows = in_weight.shape[1]
    tp_index = lax.axis_index("yl") * 2 + lax.axis_index("core")

    in_shard = jnp.concatenate([in_weight[0], in_weight[1], in_weight[2]], axis=1)
    in_full, second_full = gather_rows(
        in_shard, jnp.concatenate([out_weight.T, down_weight.T], axis=1)
    )
    out_full = second_full[:, :chan_dev]
    down_full = second_full[:, chan_dev:]
    up_gate_full = lax.all_gather(up_gate_weight, FSDP, axis=1, tiled=True)

    conv_local = lax.dynamic_slice_in_dim(conv_weight, tp_index * chan_dev, chan_dev, 1).astype(F32)
    tok_f32 = tokens.astype(F32)
    scale_one, normed_one = norm_parts(tok_f32)
    gain_one = mix_gain.astype(F32)
    mix_rows = reordered(gather_tokens((normed_one * gain_one).astype(BF16)))
    group_rows = mix_rows.shape[0]
    projected = dot(mix_rows, in_full, 1, 0).astype(BF16)
    proj_b = projected[:, :chan_dev].astype(F32)
    proj_c = projected[:, chan_dev : 2 * chan_dev].astype(F32)
    proj_x = projected[:, 2 * chan_dev :].astype(F32)
    product = proj_b * proj_x
    parity = (segments % 2).astype(F32)
    parity_row = jnp.zeros((1, chan_dev), F32).at[0, :2].set(parity[-2:])
    rim_send = jnp.concatenate([product[-2:], parity_row], axis=0)
    rim_recv = along_tokens(rim_send, 1)
    padded = jnp.concatenate([rim_recv[:2], product], axis=0)
    parity_pad = jnp.concatenate([rim_recv[2, :2], parity])
    masks = [
        (parity_pad[2 - offset : 2 - offset + group_rows] == parity).astype(F32)[:, None]
        for offset in range(3)
    ]
    conv_out = jnp.zeros_like(product)
    for offset in range(3):
        conv_out = (
            conv_out
            + conv_local[2 - offset] * masks[offset] * padded[2 - offset : 2 - offset + group_rows]
        )
    mixer_in = (proj_c * conv_out).astype(BF16)
    mixer_out = scatter_tokens(dot(restored(mixer_in), out_full, 1, 1))
    middle = tok_f32 + mixer_out
    scale_two, normed_two = norm_parts(middle)
    gain_two = ffn_gain.astype(F32)
    cot_rows = gather_tokens(after(cotangent, mix_rows))
    second = (normed_two * gain_two).astype(BF16)
    ffn_rows = gather_core(second, after(swapped(second, "yl"), up_gate_full))
    grad_hidden = dot(cot_rows, down_full, 1, 0)
    gate_val = dot(ffn_rows, up_gate_full[0], 1, 0)
    up_val = dot(ffn_rows, up_gate_full[1], 1, 0)
    sigma = jax.nn.sigmoid(gate_val)
    hidden = (gate_val * sigma * up_val).astype(BF16)
    grad_up = grad_hidden * gate_val * sigma
    grad_gate = grad_hidden * up_val * sigma * (1.0 + gate_val * (1.0 - sigma))
    grad_gate = grad_gate.astype(BF16)
    grad_up = grad_up.astype(BF16)
    grad_down = dot(z_outermost(cot_rows), hidden, 0, 0).astype(BF16)
    down_part = exchange_sum(grad_down, ("z",)).astype(BF16)
    grad_gate = after(grad_gate, grad_down)
    grad_rows_two = dot(grad_gate, up_gate_full[0], 1, 1) + dot(grad_up, up_gate_full[1], 1, 1)
    grad_gate_w = dot(
        x_outermost(after(ffn_rows, grad_rows_two)), jnp.concatenate([grad_gate, grad_up], axis=1), 0, 0
    ).astype(BF16)
    gate_part = lax.psum_scatter(grad_gate_w, "x", scatter_dimension=0, tiled=True)
    gate_part = lax.psum_scatter(gate_part, "z", scatter_dimension=0, tiled=True)
    grad_normed_two = scatter_tokens(grad_rows_two)
    gain_two_grad = jnp.sum(grad_normed_two * normed_two, axis=0)
    grad_middle = cotangent.astype(F32) + norm_back(grad_normed_two, gain_two, scale_two, normed_two)
    grad_mid_low = grad_middle.astype(BF16)
    grad_mid_far = no_sooner(swapped(grad_mid_low, "yl"), down_part)
    grad_mix_rows = reordered(gather_core(grad_mid_low, grad_mid_far))
    ffn_terms = dot(after(hidden, grad_mid_low), down_full, 1, 1)
    mixed = (middle + scatter_tokens(after(ffn_terms, grad_mix_rows))).astype(BF16)
    grad_mixer_in = dot(grad_mix_rows, out_full, 1, 0)
    grad_out_w = dot(grad_mix_rows, mixer_in, 0, 0).astype(BF16)
    grad_c = grad_mixer_in * conv_out
    grad_conv = grad_mixer_in * proj_c
    grad_padded = jnp.zeros((group_rows + 2, chan_dev), F32)
    conv_grads = []
    for offset in range(3):
        masked = masks[offset] * grad_conv
        grad_padded = grad_padded + jnp.pad(
            conv_local[2 - offset] * masked, ((2 - offset, offset), (0, 0))
        )
        conv_grads.append(jnp.sum(masked * padded[2 - offset : 2 - offset + group_rows], axis=0))
    conv_grad_local = jnp.stack([conv_grads[2], conv_grads[1], conv_grads[0]])
    rim_back = along_tokens(grad_padded[:2], -1)
    grad_product = grad_padded[2:] + jnp.pad(rim_back, ((group_rows - 2, 0), (0, 0)))
    grad_proj = jnp.concatenate(
        [
            (grad_product * proj_x).astype(BF16),
            grad_c.astype(BF16),
            (grad_product * proj_b).astype(BF16),
        ],
        axis=1,
    )
    grad_in_w = dot(mix_rows, grad_proj, 0, 0).astype(BF16)
    grad_rows_one = dot(grad_proj, in_full, 1, 1)
    gain_one_grad = jnp.sum(grad_rows_one * mix_rows.astype(F32), axis=0) / gain_one
    grad_normed_one = scatter_tokens(restored(grad_rows_one))
    input_grad = grad_middle + norm_back(grad_normed_one, gain_one, scale_one, normed_one)

    small = jnp.concatenate(
        [
            gain_one_grad.reshape(shard_rows, -1),
            gain_two_grad.reshape(shard_rows, -1),
            conv_grad_local.reshape(shard_rows, -1),
        ],
        axis=1,
    )
    small = jnp.pad(small, ((0, 0), (0, 128 - small.shape[1]))).astype(BF16)
    small = jnp.broadcast_to(small, (32,) + small.shape).reshape(width, 128)
    last_grad = jnp.concatenate([grad_out_w, grad_in_w, small], axis=1)
    last_shard = exchange_sum(last_grad, FSDP)
    out_shard = last_shard[:, :chan_dev]
    in_shard = last_shard[:, chan_dev : 4 * chan_dev]
    sums = last_shard[:, 4 * chan_dev : 4 * chan_dev + 128]
    per = width // shard_rows
    conv_sum = sums[:, 2 * per : 2 * per + 3 * chan_dev // shard_rows].reshape(3, chan_dev)
    conv_sum = lax.dynamic_update_slice_in_dim(
        jnp.zeros((3, width), F32), conv_sum, tp_index * chan_dev, 1
    )
    sums = jnp.concatenate(
        [sums[:, :per].reshape(1, width), sums[:, per : 2 * per].reshape(1, width), conv_sum]
    )
    sums = no_sooner(sums, gate_part)
    sums = sums + swapped(sums, "core")
    sums = sums + swapped(sums, "yl")

    down_pair = ring_scatter(down_part.reshape(2, 4, shard_rows, -1), "x", 1, grad_in_w)
    ffn_part = jnp.concatenate(
        [gate_part.reshape(2, shard_rows, -1), down_pair.astype(BF16)], axis=2
    )
    me = lax.axis_index("yh")
    ffn_far = swapped(take(ffn_part, 0, 1 - me), "yh")
    ffn_grad_shard = take(ffn_part, 0, me).astype(F32) + ffn_far.astype(F32)
    down_shard = ffn_grad_shard[:, 2 * hidden_dev :]
    gate_shard = ffn_grad_shard[:, :hidden_dev]
    up_shard = ffn_grad_shard[:, hidden_dev : 2 * hidden_dev]
    return (
        mixed,
        input_grad,
        sums[0],
        jnp.stack([in_shard[:, i * chan_dev : (i + 1) * chan_dev] for i in range(3)]),
        sums[2:],
        out_shard.T,
        sums[1],
        jnp.stack([gate_shard, up_shard]),
        down_shard.T,
    )


def solution(mesh):
    fine = Mesh(mesh.devices.reshape(2, 4, 4, 2, 2), ALL)
    placed = (
        P(ALL, None),
        P(FSDP),
        P(),
        P(None, FSDP, TP),
        P(),
        P(TP, FSDP),
        P(),
        P(None, FSDP, TP),
        P(TP, FSDP),
        P(ALL, None),
    )
    return jax.shard_map(
        local,
        mesh=fine,
        in_specs=placed,
        out_specs=(
            P(ALL, None),
            P(ALL, None),
            P(),
            P(None, FSDP, TP),
            P(),
            P(TP, FSDP),
            P(),
            P(None, FSDP, TP),
            P(TP, FSDP),
        ),
        check_vma=False,
    )
```

```python
import jax
import jax.numpy as jnp
from jax import lax
from jax.sharding import Mesh, PartitionSpec as P

EPSILON = 1e-05
F32 = jnp.float32
BF16 = jnp.bfloat16
FSDP = ("yh", "z", "x")
TP = ("yl", "core")
ALL = FSDP + TP


def dot(lhs, rhs, lhs_dim, rhs_dim):
    return lax.dot_general(
        lhs, rhs, (((lhs_dim,), (rhs_dim,)), ((), ())), preferred_element_type=F32
    )


def shifted(value, axis, by):
    size = lax.axis_size(axis)
    return lax.ppermute(value, axis, [(i, (i + by) % size) for i in range(size)])


def swapped(value, axis):
    return lax.ppermute(value, axis, [(0, 1), (1, 0)])


def norm_parts(values):
    scale = lax.rsqrt(jnp.mean(values * values, axis=-1, keepdims=True) + EPSILON)
    return (scale, values * scale)


def norm_back(grad_out, gain, scale, normed):
    grad_norm = grad_out * gain
    return scale * (grad_norm - normed * jnp.mean(grad_norm * normed, axis=-1, keepdims=True))


def after(value, *earlier):
    return lax.optimization_barrier((value,) + earlier)[0]


def no_sooner(value, earlier):
    corner = lax.slice(earlier, (0,) * earlier.ndim, (1,) * earlier.ndim).reshape(())
    return value + jnp.minimum(jnp.abs(corner), 0).astype(value.dtype)


def put(block, whole, dim, index):
    return lax.dynamic_update_slice_in_dim(whole, jnp.expand_dims(block, dim), index, dim)


def take(whole, dim, index):
    return lax.dynamic_index_in_dim(whole, index, dim, keepdims=False)


def ring_gather(block, axis, dim):
    me = lax.axis_index(axis)
    whole = jnp.zeros(block.shape[:dim] + (4,) + block.shape[dim:], block.dtype)
    whole = put(block, whole, dim, me)
    for by in (1, 3, 2):
        whole = put(shifted(block, axis, by), whole, dim, (me - by) % 4)
    return whole


def ring_gather_passing(block, axis, dim):
    me = lax.axis_index(axis)
    before = shifted(block, axis, 1)
    behind = shifted(block, axis, -1)
    far = jnp.concatenate([shifted(before[:1], axis, 1), shifted(behind[1:], axis, -1)])
    whole = jnp.zeros(block.shape[:dim] + (4,) + block.shape[dim:], block.dtype)
    for value, by in ((block, 0), (before, 3), (behind, 1), (far, 2)):
        whole = put(value, whole, dim, (me + by) % 4)
    return whole


def pair_rows(shard):
    other = swapped(shard, "yh")
    first = lax.axis_index("yh") == 0
    return jnp.stack([jnp.where(first, shard, other), jnp.where(first, other, shard)])


def gather_rows(first, second, pair):
    columns = first.shape[1]
    one = ring_gather(ring_gather(pair[:, :, :columns], "z", 1), "x", 2)
    two = ring_gather_passing(ring_gather(pair[:, :, columns:], "x", 1), "z", 1)
    return one.reshape(-1, columns), two.reshape(-1, second.shape[1])


def ring_scatter(whole, axis, dim, earlier):
    me = lax.axis_index(axis)
    total = take(whole, dim, me).astype(F32)
    for by in (1, 3, 2):
        part = no_sooner(take(whole, dim, (me + by) % 4), earlier)
        total = total + shifted(part, axis, by).astype(F32)
    return total


def exchange_sum(whole, axes):
    count = 1
    for axis in axes:
        count *= lax.axis_size(axis)
    parts = lax.all_to_all(whole.reshape(count, -1, whole.shape[1]), axes, 0, 0)
    return jnp.sum(parts.astype(F32), axis=0)


def x_outermost(rows):
    parts = rows.reshape(rows.shape[0], 2, 4, 4, -1).transpose(0, 3, 2, 1, 4)
    return parts.reshape(rows.shape)


def z_outermost(rows):
    parts = rows.reshape(rows.shape[0], 2, 4, 4, -1).swapaxes(1, 2)
    return parts.reshape(rows.shape)


def gather_tokens(block):
    return gather_core(block, swapped(block, "yl"))


def gather_core(block, far):
    pair = jnp.concatenate([block, far])
    return jnp.concatenate([pair, swapped(pair, "core")])


def scatter_tokens(terms, earlier=None):
    half = terms.shape[0] // 2
    pair = terms[:half].astype(F32) + swapped(terms[half:].astype(BF16), "core").astype(F32)
    rows = half // 2
    far = swapped(pair[rows:].astype(BF16), "yl")
    if earlier is not None:
        far = no_sooner(far, earlier)
    return pair[:rows] + far.astype(F32)


def reordered(rows):
    blocks = rows.reshape(4, -1, rows.shape[1])
    me = lax.axis_index("core") * 2 + lax.axis_index("yl")
    return jnp.concatenate([take(blocks, 0, me ^ other) for other in (0, 2, 1, 3)])


def restored(rows):
    blocks = rows.reshape(4, -1, rows.shape[1])
    me = lax.axis_index("yl") * 2 + lax.axis_index("core")
    return jnp.concatenate([take(blocks, 0, me ^ other) for other in (0, 2, 1, 3)])


def along_tokens(value, by):
    pairs = [(i, i + by) for i in range(32) if 0 <= i + by < 32]
    return lax.ppermute(value, FSDP, pairs)


def local(
    tokens,
    segments,
    mix_gain,
    in_weight,
    conv_weight,
    out_weight,
    ffn_gain,
    up_gate_weight,
    down_weight,
    cotangent,
):
    width = tokens.shape[1]
    chan_dev = in_weight.shape[2]
    hidden_dev = up_gate_weight.shape[2]
    shard_rows = in_weight.shape[1]
    tp_index = lax.axis_index("yl") * 2 + lax.axis_index("core")

    in_shard = jnp.concatenate([in_weight[0], in_weight[1], in_weight[2]], axis=1)
    second_shard = jnp.concatenate([out_weight.T, down_weight.T], axis=1)
    mixer_pair = pair_rows(jnp.concatenate([in_shard, second_shard], axis=1))
    in_full, second_full = gather_rows(in_shard, second_shard, mixer_pair)
    out_full = second_full[:, :chan_dev]
    down_full = second_full[:, chan_dev:]
    up_gate_full = lax.all_gather(up_gate_weight, FSDP, axis=1, tiled=True)

    conv_local = lax.dynamic_slice_in_dim(conv_weight, tp_index * chan_dev, chan_dev, 1).astype(F32)
    tok_f32 = no_sooner(tokens, mixer_pair).astype(F32)
    scale_one, normed_one = norm_parts(tok_f32)
    gain_one = mix_gain.astype(F32)
    mix_rows = reordered(gather_tokens((normed_one * gain_one).astype(BF16)))
    group_rows = mix_rows.shape[0]
    projected = dot(mix_rows, in_full, 1, 0).astype(BF16)
    proj_b = projected[:, :chan_dev].astype(F32)
    proj_c = projected[:, chan_dev : 2 * chan_dev].astype(F32)
    proj_x = projected[:, 2 * chan_dev :].astype(F32)
    product = proj_b * proj_x
    parity = (segments % 2).astype(F32)
    parity_row = jnp.zeros((1, chan_dev), F32).at[0, :2].set(parity[-2:])
    rim_send = jnp.concatenate([product[-2:], parity_row], axis=0)
    rim_recv = along_tokens(rim_send, 1)
    padded = jnp.concatenate([rim_recv[:2], product], axis=0)
    parity_pad = jnp.concatenate([rim_recv[2, :2], parity])
    masks = [
        (parity_pad[2 - offset : 2 - offset + group_rows] == parity).astype(F32)[:, None]
        for offset in range(3)
    ]
    conv_out = jnp.zeros_like(product)
    for offset in range(3):
        conv_out = (
            conv_out
            + conv_local[2 - offset] * masks[offset] * padded[2 - offset : 2 - offset + group_rows]
        )
    mixer_in = (proj_c * conv_out).astype(BF16)
    mixer_out = scatter_tokens(dot(restored(mixer_in), out_full, 1, 1))
    middle = tok_f32 + mixer_out
    scale_two, normed_two = norm_parts(middle)
    gain_two = ffn_gain.astype(F32)
    cot_rows = gather_tokens(after(cotangent, mix_rows))
    second = (normed_two * gain_two).astype(BF16)
    ffn_rows = gather_core(second, after(swapped(second, "yl"), up_gate_full))
    grad_hidden = dot(cot_rows, down_full, 1, 0)
    gate_val = dot(ffn_rows, up_gate_full[0], 1, 0)
    up_val = dot(ffn_rows, up_gate_full[1], 1, 0)
    sigma = jax.nn.sigmoid(gate_val)
    hidden = (gate_val * sigma * up_val).astype(BF16)
    grad_up = grad_hidden * gate_val * sigma
    grad_gate = grad_hidden * up_val * sigma * (1.0 + gate_val * (1.0 - sigma))
    grad_gate = grad_gate.astype(BF16)
    grad_up = grad_up.astype(BF16)
    grad_down = dot(z_outermost(cot_rows), hidden, 0, 0).astype(BF16)
    down_part = exchange_sum(grad_down, ("z",)).astype(BF16)
    grad_gate = after(grad_gate, grad_down)
    grad_rows_two = dot(grad_gate, up_gate_full[0], 1, 1) + dot(grad_up, up_gate_full[1], 1, 1)
    grad_gate_w = dot(
        x_outermost(after(ffn_rows, grad_rows_two)), jnp.concatenate([grad_gate, grad_up], axis=1), 0, 0
    ).astype(BF16)
    gate_part = lax.psum_scatter(grad_gate_w, "x", scatter_dimension=0, tiled=True)
    gate_part = lax.psum_scatter(gate_part, "z", scatter_dimension=0, tiled=True)
    grad_normed_two = scatter_tokens(grad_rows_two)
    gain_two_grad = jnp.sum(grad_normed_two * normed_two, axis=0)
    grad_middle = cotangent.astype(F32) + norm_back(grad_normed_two, gain_two, scale_two, normed_two)
    grad_mid_low = grad_middle.astype(BF16)
    grad_mid_far = no_sooner(swapped(grad_mid_low, "yl"), down_part)
    grad_mix_rows = reordered(gather_core(grad_mid_low, grad_mid_far))
    ffn_terms = dot(after(hidden, grad_mid_low), down_full, 1, 1)
    mixed = (middle + scatter_tokens(after(ffn_terms, grad_mix_rows))).astype(BF16)
    grad_mixer_in = dot(grad_mix_rows, out_full, 1, 0)
    grad_out_w = dot(grad_mix_rows, mixer_in, 0, 0).astype(BF16)
    grad_c = grad_mixer_in * conv_out
    grad_conv = grad_mixer_in * proj_c
    grad_padded = jnp.zeros((group_rows + 2, chan_dev), F32)
    conv_grads = []
    for offset in range(3):
        masked = masks[offset] * grad_conv
        grad_padded = grad_padded + jnp.pad(
            conv_local[2 - offset] * masked, ((2 - offset, offset), (0, 0))
        )
        conv_grads.append(jnp.sum(masked * padded[2 - offset : 2 - offset + group_rows], axis=0))
    conv_grad_local = jnp.stack([conv_grads[2], conv_grads[1], conv_grads[0]])
    rim_back = along_tokens(grad_padded[:2], -1)
    grad_product = grad_padded[2:] + jnp.pad(rim_back, ((group_rows - 2, 0), (0, 0)))
    grad_proj = jnp.concatenate(
        [
            (grad_product * proj_x).astype(BF16),
            grad_c.astype(BF16),
            (grad_product * proj_b).astype(BF16),
        ],
        axis=1,
    )
    grad_in_w = dot(mix_rows, grad_proj, 0, 0).astype(BF16)
    grad_rows_one = dot(grad_proj, in_full, 1, 1)
    gain_one_grad = jnp.sum(grad_rows_one * mix_rows.astype(F32), axis=0) / gain_one
    grad_normed_one = scatter_tokens(restored(grad_rows_one))
    input_grad = grad_middle + norm_back(grad_normed_one, gain_one, scale_one, normed_one)

    small = jnp.concatenate(
        [
            gain_one_grad.reshape(shard_rows, -1),
            gain_two_grad.reshape(shard_rows, -1),
            conv_grad_local.reshape(shard_rows, -1),
        ],
        axis=1,
    )
    small = jnp.pad(small, ((0, 0), (0, 128 - small.shape[1]))).astype(BF16)
    small = jnp.broadcast_to(small, (32,) + small.shape).reshape(width, 128)
    last_grad = jnp.concatenate([grad_out_w, grad_in_w, small], axis=1)
    last_shard = exchange_sum(last_grad, FSDP)
    out_shard = last_shard[:, :chan_dev]
    in_shard = last_shard[:, chan_dev : 4 * chan_dev]
    sums = last_shard[:, 4 * chan_dev : 4 * chan_dev + 128]
    per = width // shard_rows
    conv_sum = sums[:, 2 * per : 2 * per + 3 * chan_dev // shard_rows].reshape(3, chan_dev)
    conv_sum = lax.dynamic_update_slice_in_dim(
        jnp.zeros((3, width), F32), conv_sum, tp_index * chan_dev, 1
    )
    sums = jnp.concatenate(
        [sums[:, :per].reshape(1, width), sums[:, per : 2 * per].reshape(1, width), conv_sum]
    )
    sums = no_sooner(sums, gate_part)
    sums = sums + swapped(sums, "core")
    sums = sums + swapped(sums, "yl")

    down_pair = ring_scatter(down_part.reshape(2, 4, shard_rows, -1), "x", 1, grad_in_w)
    ffn_part = jnp.concatenate(
        [gate_part.reshape(2, shard_rows, -1), down_pair.astype(BF16)], axis=2
    )
    me = lax.axis_index("yh")
    ffn_far = swapped(take(ffn_part, 0, 1 - me), "yh")
    ffn_grad_shard = take(ffn_part, 0, me).astype(F32) + ffn_far.astype(F32)
    down_shard = ffn_grad_shard[:, 2 * hidden_dev :]
    gate_shard = ffn_grad_shard[:, :hidden_dev]
    up_shard = ffn_grad_shard[:, hidden_dev : 2 * hidden_dev]
    return (
        mixed,
        input_grad,
        sums[0],
        jnp.stack([in_shard[:, i * chan_dev : (i + 1) * chan_dev] for i in range(3)]),
        sums[2:],
        out_shard.T,
        sums[1],
        jnp.stack([gate_shard, up_shard]),
        down_shard.T,
    )


def solution(mesh):
    fine = Mesh(mesh.devices.reshape(2, 4, 4, 2, 2), ALL)
    placed = (
        P(ALL, None),
        P(FSDP),
        P(),
        P(None, FSDP, TP),
        P(),
        P(TP, FSDP),
        P(),
        P(None, FSDP, TP),
        P(TP, FSDP),
        P(ALL, None),
    )
    return jax.shard_map(
        local,
        mesh=fine,
        in_specs=placed,
        out_specs=(
            P(ALL, None),
            P(ALL, None),
            P(),
            P(None, FSDP, TP),
            P(),
            P(TP, FSDP),
            P(),
            P(None, FSDP, TP),
            P(TP, FSDP),
        ),
        check_vma=False,
    )
```

```python
import jax
import jax.numpy as jnp
from jax import lax
from jax.sharding import Mesh, PartitionSpec as P

EPSILON = 1e-05
F32 = jnp.float32
BF16 = jnp.bfloat16
FSDP = ("yh", "z", "x")
TP = ("yl", "core")
ALL = FSDP + TP


def dot(lhs, rhs, lhs_dim, rhs_dim):
    return lax.dot_general(
        lhs, rhs, (((lhs_dim,), (rhs_dim,)), ((), ())), preferred_element_type=F32
    )


def shifted(value, axis, by):
    size = lax.axis_size(axis)
    return lax.ppermute(value, axis, [(i, (i + by) % size) for i in range(size)])


def swapped(value, axis):
    return lax.ppermute(value, axis, [(0, 1), (1, 0)])


def norm_parts(values):
    scale = lax.rsqrt(jnp.mean(values * values, axis=-1, keepdims=True) + EPSILON)
    return (scale, values * scale)


def norm_back(grad_out, gain, scale, normed):
    grad_norm = grad_out * gain
    return scale * (grad_norm - normed * jnp.mean(grad_norm * normed, axis=-1, keepdims=True))


def after(value, *earlier):
    return lax.optimization_barrier((value,) + earlier)[0]


def no_sooner(value, earlier):
    corner = lax.slice(earlier, (0,) * earlier.ndim, (1,) * earlier.ndim).reshape(())
    return value + jnp.minimum(jnp.abs(corner), 0).astype(value.dtype)


def put(block, whole, dim, index):
    return lax.dynamic_update_slice_in_dim(whole, jnp.expand_dims(block, dim), index, dim)


def take(whole, dim, index):
    return lax.dynamic_index_in_dim(whole, index, dim, keepdims=False)


def ring_gather(block, axis, dim):
    me = lax.axis_index(axis)
    whole = jnp.zeros(block.shape[:dim] + (4,) + block.shape[dim:], block.dtype)
    whole = put(block, whole, dim, me)
    for by in (1, 3, 2):
        whole = put(shifted(block, axis, by), whole, dim, (me - by) % 4)
    return whole


def ring_gather_passing(block, axis, dim):
    me = lax.axis_index(axis)
    before = shifted(block, axis, 1)
    behind = shifted(block, axis, -1)
    far = jnp.concatenate([shifted(before[:1], axis, 1), shifted(behind[1:], axis, -1)])
    whole = jnp.zeros(block.shape[:dim] + (4,) + block.shape[dim:], block.dtype)
    for value, by in ((block, 0), (before, 3), (behind, 1), (far, 2)):
        whole = put(value, whole, dim, (me + by) % 4)
    return whole


def pair_rows(shard):
    other = swapped(shard, "yh")
    first = lax.axis_index("yh") == 0
    return jnp.stack([jnp.where(first, shard, other), jnp.where(first, other, shard)])


def gather_rows(first, second, pair):
    columns = first.shape[1]
    one = ring_gather(ring_gather(pair[:, :, :columns], "z", 1), "x", 2)
    two = ring_gather_passing(ring_gather(pair[:, :, columns:], "x", 1), "z", 1)
    return one.reshape(-1, columns), two.reshape(-1, second.shape[1])


def ring_scatter(whole, axis, dim, earlier):
    me = lax.axis_index(axis)
    total = take(whole, dim, me).astype(F32)
    for by in (1, 3, 2):
        part = no_sooner(take(whole, dim, (me + by) % 4), earlier)
        total = total + shifted(part, axis, by).astype(F32)
    return total


def exchange_sum(whole, axes):
    count = 1
    for axis in axes:
        count *= lax.axis_size(axis)
    parts = lax.all_to_all(whole.reshape(count, -1, whole.shape[1]), axes, 0, 0)
    return jnp.sum(parts.astype(F32), axis=0)


def x_outermost(rows):
    parts = rows.reshape(rows.shape[0], 2, 4, 4, -1).transpose(0, 3, 2, 1, 4)
    return parts.reshape(rows.shape)


def z_outermost(rows):
    parts = rows.reshape(rows.shape[0], 2, 4, 4, -1).swapaxes(1, 2)
    return parts.reshape(rows.shape)


def gather_tokens(block):
    return gather_core(block, swapped(block, "yl"))


def gather_core(block, far):
    pair = jnp.concatenate([block, far])
    return jnp.concatenate([pair, swapped(pair, "core")])


def scatter_tokens(terms, earlier=None):
    half = terms.shape[0] // 2
    pair = terms[:half].astype(F32) + swapped(terms[half:].astype(BF16), "core").astype(F32)
    rows = half // 2
    far = swapped(pair[rows:].astype(BF16), "yl")
    if earlier is not None:
        far = no_sooner(far, earlier)
    return pair[:rows] + far.astype(F32)


def reordered(rows):
    blocks = rows.reshape(4, -1, rows.shape[1])
    me = lax.axis_index("core") * 2 + lax.axis_index("yl")
    return jnp.concatenate([take(blocks, 0, me ^ other) for other in (0, 2, 1, 3)])


def restored(rows):
    blocks = rows.reshape(4, -1, rows.shape[1])
    me = lax.axis_index("yl") * 2 + lax.axis_index("core")
    return jnp.concatenate([take(blocks, 0, me ^ other) for other in (0, 2, 1, 3)])


def along_tokens(value, by):
    pairs = [(i, i + by) for i in range(32) if 0 <= i + by < 32]
    return lax.ppermute(value, FSDP, pairs)


def local(
    tokens,
    segments,
    mix_gain,
    in_weight,
    conv_weight,
    out_weight,
    ffn_gain,
    up_gate_weight,
    down_weight,
    cotangent,
):
    width = tokens.shape[1]
    chan_dev = in_weight.shape[2]
    hidden_dev = up_gate_weight.shape[2]
    shard_rows = in_weight.shape[1]
    tp_index = lax.axis_index("yl") * 2 + lax.axis_index("core")

    in_shard = jnp.concatenate([in_weight[0], in_weight[1], in_weight[2]], axis=1)
    second_shard = jnp.concatenate([out_weight.T, down_weight.T], axis=1)
    mixer_pair = pair_rows(jnp.concatenate([in_shard, second_shard], axis=1))
    in_full, second_full = gather_rows(in_shard, second_shard, mixer_pair)
    out_full = second_full[:, :chan_dev]
    down_full = second_full[:, chan_dev:]
    up_gate_full = lax.all_gather(up_gate_weight, FSDP, axis=1, tiled=True)

    conv_local = lax.dynamic_slice_in_dim(conv_weight, tp_index * chan_dev, chan_dev, 1).astype(F32)
    tok_f32 = no_sooner(tokens, mixer_pair).astype(F32)
    scale_one, normed_one = norm_parts(tok_f32)
    gain_one = mix_gain.astype(F32)
    mix_rows = reordered(gather_tokens((normed_one * gain_one).astype(BF16)))
    group_rows = mix_rows.shape[0]
    projected = dot(mix_rows, in_full, 1, 0).astype(BF16)
    proj_b = projected[:, :chan_dev].astype(F32)
    proj_c = projected[:, chan_dev : 2 * chan_dev].astype(F32)
    proj_x = projected[:, 2 * chan_dev :].astype(F32)
    product = proj_b * proj_x
    parity = (segments % 2).astype(F32)
    parity_row = jnp.zeros((1, chan_dev), F32).at[0, :2].set(parity[-2:])
    rim_send = jnp.concatenate([product[-2:], parity_row], axis=0)
    rim_recv = along_tokens(rim_send, 1)
    padded = jnp.concatenate([rim_recv[:2], product], axis=0)
    parity_pad = jnp.concatenate([rim_recv[2, :2], parity])
    masks = [
        (parity_pad[2 - offset : 2 - offset + group_rows] == parity).astype(F32)[:, None]
        for offset in range(3)
    ]
    conv_out = jnp.zeros_like(product)
    for offset in range(3):
        conv_out = (
            conv_out
            + conv_local[2 - offset] * masks[offset] * padded[2 - offset : 2 - offset + group_rows]
        )
    mixer_in = (proj_c * conv_out).astype(BF16)
    mixer_out = scatter_tokens(dot(restored(mixer_in), out_full, 1, 1))
    middle = tok_f32 + mixer_out
    scale_two, normed_two = norm_parts(middle)
    gain_two = ffn_gain.astype(F32)
    cot_rows = gather_tokens(after(cotangent, mix_rows))
    second = (normed_two * gain_two).astype(BF16)
    ffn_rows = gather_core(second, after(swapped(second, "yl"), up_gate_full))
    grad_hidden = dot(cot_rows, down_full, 1, 0)
    gate_val = dot(ffn_rows, up_gate_full[0], 1, 0)
    up_val = dot(ffn_rows, up_gate_full[1], 1, 0)
    sigma = jax.nn.sigmoid(gate_val)
    hidden = (gate_val * sigma * up_val).astype(BF16)
    grad_up = grad_hidden * gate_val * sigma
    grad_gate = grad_hidden * up_val * sigma * (1.0 + gate_val * (1.0 - sigma))
    grad_gate = grad_gate.astype(BF16)
    grad_up = grad_up.astype(BF16)
    grad_down = dot(z_outermost(cot_rows), hidden, 0, 0).astype(BF16)
    down_part = exchange_sum(grad_down, ("z",)).astype(BF16)
    grad_gate = after(grad_gate, grad_down)
    grad_rows_two = dot(grad_gate, up_gate_full[0], 1, 1) + dot(grad_up, up_gate_full[1], 1, 1)
    grad_gate_w = dot(
        x_outermost(after(ffn_rows, grad_rows_two)), jnp.concatenate([grad_gate, grad_up], axis=1), 0, 0
    ).astype(BF16)
    gate_part = lax.psum_scatter(grad_gate_w, "x", scatter_dimension=0, tiled=True)
    gate_part = lax.psum_scatter(gate_part, "z", scatter_dimension=0, tiled=True)
    grad_normed_two = scatter_tokens(grad_rows_two)
    gain_two_grad = jnp.sum(grad_normed_two * normed_two, axis=0)
    grad_middle = cotangent.astype(F32) + norm_back(grad_normed_two, gain_two, scale_two, normed_two)
    grad_mid_low = grad_middle.astype(BF16)
    grad_mid_far = after(swapped(grad_mid_low, "yl"), down_part)
    grad_mix_rows = reordered(gather_core(grad_mid_low, grad_mid_far))
    ffn_terms = dot(after(hidden, grad_mid_low), down_full, 1, 1)
    mixed = (middle + scatter_tokens(after(ffn_terms, grad_mix_rows))).astype(BF16)
    grad_mixer_in = dot(grad_mix_rows, out_full, 1, 0)
    grad_out_w = dot(grad_mix_rows, mixer_in, 0, 0).astype(BF16)
    grad_c = grad_mixer_in * conv_out
    grad_conv = grad_mixer_in * proj_c
    grad_padded = jnp.zeros((group_rows + 2, chan_dev), F32)
    conv_grads = []
    for offset in range(3):
        masked = masks[offset] * grad_conv
        grad_padded = grad_padded + jnp.pad(
            conv_local[2 - offset] * masked, ((2 - offset, offset), (0, 0))
        )
        conv_grads.append(jnp.sum(masked * padded[2 - offset : 2 - offset + group_rows], axis=0))
    conv_grad_local = jnp.stack([conv_grads[2], conv_grads[1], conv_grads[0]])
    rim_back = along_tokens(grad_padded[:2], -1)
    grad_product = grad_padded[2:] + jnp.pad(rim_back, ((group_rows - 2, 0), (0, 0)))
    grad_proj = jnp.concatenate(
        [
            (grad_product * proj_x).astype(BF16),
            grad_c.astype(BF16),
            (grad_product * proj_b).astype(BF16),
        ],
        axis=1,
    )
    grad_in_w = dot(mix_rows, grad_proj, 0, 0).astype(BF16)
    grad_rows_one = dot(grad_proj, in_full, 1, 1)
    gain_one_grad = jnp.sum(grad_rows_one * mix_rows.astype(F32), axis=0) / gain_one
    grad_normed_one = scatter_tokens(restored(grad_rows_one))
    input_grad = grad_middle + norm_back(grad_normed_one, gain_one, scale_one, normed_one)

    small = jnp.concatenate(
        [
            gain_one_grad.reshape(shard_rows, -1),
            gain_two_grad.reshape(shard_rows, -1),
            conv_grad_local.reshape(shard_rows, -1),
        ],
        axis=1,
    )
    small = jnp.pad(small, ((0, 0), (0, 128 - small.shape[1]))).astype(BF16)
    small = jnp.broadcast_to(small, (32,) + small.shape).reshape(width, 128)
    last_grad = jnp.concatenate([grad_out_w, grad_in_w, small], axis=1)
    last_shard = exchange_sum(last_grad, FSDP)
    out_shard = last_shard[:, :chan_dev]
    in_shard = last_shard[:, chan_dev : 4 * chan_dev]
    sums = last_shard[:, 4 * chan_dev : 4 * chan_dev + 128]
    per = width // shard_rows
    conv_sum = sums[:, 2 * per : 2 * per + 3 * chan_dev // shard_rows].reshape(3, chan_dev)
    conv_sum = lax.dynamic_update_slice_in_dim(
        jnp.zeros((3, width), F32), conv_sum, tp_index * chan_dev, 1
    )
    sums = jnp.concatenate(
        [sums[:, :per].reshape(1, width), sums[:, per : 2 * per].reshape(1, width), conv_sum]
    )
    sums = after(sums, gate_part)
    sums = sums + swapped(sums, "core")
    sums = sums + swapped(sums, "yl")

    down_pair = ring_scatter(down_part.reshape(2, 4, shard_rows, -1), "x", 1, grad_in_w)
    ffn_part = jnp.concatenate(
        [gate_part.reshape(2, shard_rows, -1), down_pair.astype(BF16)], axis=2
    )
    me = lax.axis_index("yh")
    ffn_far = swapped(take(ffn_part, 0, 1 - me), "yh")
    ffn_grad_shard = take(ffn_part, 0, me).astype(F32) + ffn_far.astype(F32)
    down_shard = ffn_grad_shard[:, 2 * hidden_dev :]
    gate_shard = ffn_grad_shard[:, :hidden_dev]
    up_shard = ffn_grad_shard[:, hidden_dev : 2 * hidden_dev]
    return (
        mixed,
        input_grad,
        sums[0],
        jnp.stack([in_shard[:, i * chan_dev : (i + 1) * chan_dev] for i in range(3)]),
        sums[2:],
        out_shard.T,
        sums[1],
        jnp.stack([gate_shard, up_shard]),
        down_shard.T,
    )


def solution(mesh):
    fine = Mesh(mesh.devices.reshape(2, 4, 4, 2, 2), ALL)
    placed = (
        P(ALL, None),
        P(FSDP),
        P(),
        P(None, FSDP, TP),
        P(),
        P(TP, FSDP),
        P(),
        P(None, FSDP, TP),
        P(TP, FSDP),
        P(ALL, None),
    )
    return jax.shard_map(
        local,
        mesh=fine,
        in_specs=placed,
        out_specs=(
            P(ALL, None),
            P(ALL, None),
            P(),
            P(None, FSDP, TP),
            P(),
            P(TP, FSDP),
            P(),
            P(None, FSDP, TP),
            P(TP, FSDP),
        ),
        check_vma=False,
    )
```
